256 devices in a mesh: sub: 4 (over y_hi, core), row: 8 (over z), col: 8 (over y_lo, x).
Axes of the slice: x: 4, y: 4 (y_hi: 2, y_lo: 2; y = y_hi * 2 + y_lo), z: 8, core: 2. Of those that a mesh axis runs over, the one named last changes fastest.
Arguments:
- front: float32 [8192, 8192], P('row', ('sub', 'col')), may hold values from -3072 to 5120, as said below
- children: float32 [8, 2048, 8192], P('sub', 'row', 'col'), may hold values from -1 to 1, as said below
- child_map: int32 [8, 16], replicated, may hold values from 0 to 63, as said below
Outputs:
- factored: float32 [8192, 8192], P('row', ('sub', 'col'))
The draws below stay inside these ranges and needn't reach their ends.
Inputs may be any that keep to these rules, and one draw needn't show every extreme that they name: For each child k the entries child_map[k, b] are distinct, and child_map[k, b] % 8 == b // 2. The entries of front in the rows and columns of front blocks below 8, in front order, form a symmetric matrix whose smallest eigenvalue is at least 1024. Entries of children in columns that stand for front column blocks below 8 lie within -0.0625 to 0.0625.
All inputs are finite; a program needn't handle non-finite values.
Results may differ from the reference program's by a relative error of at most 0.00009.
Values sent between devices are 32-bit elements; how exact they have to be, the bound alone decides.
No kernel may reach another device: no remote copies, remote signals or barrier semaphores. Data moves between devices by JAX's collectives and lax.ppermute only.
A program may use at most 128 MiB of HBM per device.

```python
import jax
import jax.numpy as jnp
from jax import lax

BLK = 128
CBD = 2
PB = 8
MBR = 2
KIDS = 8
NRW = 8
NSB = 4
NCL = 8
NCG = 32
NB = 64
RBD = 8
NF = 8192
WCOL = 256
PW = 1024
MB = 16
MC = 2048


def draw_front(key, part):
    key = jax.random.fold_in(key, 11)
    key_list = jax.random.split(key, 5)
    positions = jnp.arange(NF, dtype=jnp.int32)
    blocks = positions // BLK
    offsets = positions % BLK
    row_front = (blocks % RBD * NRW + blocks // RBD) * BLK + offsets
    col_front = (blocks % CBD * NCG + blocks // CBD) * BLK + offsets
    in_rows = (row_front < PW)[:, None]
    in_cols = (col_front < PW)[None, :]
    mixing = jax.random.normal(key_list[0], (PW, PW), jnp.float32)
    row_scale = jax.random.uniform(key_list[1], (PW, 1), jnp.float32, 0.8, 1.2)
    drawn_part = jnp.clip(jax.random.normal(key_list[3], (NF, NF), jnp.float32), -4.0, 4.0)
    mixing = mixing * lax.rsqrt(jnp.mean(mixing * mixing, axis=1, keepdims=True) + 1e-06)
    scaled = mixing * row_scale
    gram = jnp.dot(scaled, scaled.T, precision=lax.Precision.HIGHEST, preferred_element_type=jnp.float32)
    lift = PW * (1.0 + jax.random.uniform(key_list[4], (PW,), jnp.float32))
    base = gram + jnp.eye(PW, dtype=jnp.float32) * lift[None, :]
    rows_pick = jnp.minimum(row_front, PW - 1).astype(jnp.int32)
    cols_pick = jnp.minimum(col_front, PW - 1).astype(jnp.int32)
    corner = jnp.take(jnp.take(base, rows_pick, axis=0), cols_pick, axis=1)
    outer_part = jnp.where(in_cols, 5.0 * drawn_part, drawn_part)
    return jnp.where(in_rows & in_cols, corner, outer_part)


def draw_children(key, part):
    key = jax.random.fold_in(key, 23)
    spread = jax.random.uniform(key, (KIDS, MC, NF), jnp.float32, -1.0, 1.0)
    columns = jnp.arange(NF, dtype=jnp.int32)
    owner_ids = columns // WCOL % NSB * NCL + columns // (NSB * WCOL)
    leading = columns % WCOL // BLK == 0
    in_panel = leading & (owner_ids < PB)
    return spread * jnp.where(in_panel, 0.0625, 1.0)[None, None, :]


def draw_child_map(key, part):
    key = jax.random.fold_in(key, 37)
    kid_ids = jnp.arange(KIDS, dtype=jnp.int32)[:, None, None]
    row_ids = jnp.arange(NRW, dtype=jnp.int32)[None, :, None]
    slot_ids = jnp.arange(RBD, dtype=jnp.int32)[None, None, :]
    scores = jax.random.randint(key, (KIDS, NRW, RBD), 0, 1 << 20, dtype=jnp.int32) * RBD + slot_ids
    first_pick = (kid_ids == 0) & (row_ids == 0) & (slot_ids == 0)
    last_pick = (kid_ids == KIDS - 1) & (row_ids == NRW - 1) & (slot_ids == RBD - 1)
    scores = jnp.where(first_pick | last_pick, -1, scores)
    ranking = jnp.argsort(scores, axis=2)
    chosen = ranking[:, :, :MBR].astype(jnp.int32)
    blocks = chosen * NRW + row_ids
    return blocks.reshape(KIDS, MB).astype(jnp.int32)


def setup_inputs(seed: int = 0) -> dict:
    keys = jax.random.split(jax.random.key(seed), 4)
    return {
        "front": draw_front(jax.random.fold_in(keys[3], 71), 0),
        "children": draw_children(jax.random.fold_in(keys[3], 71), 0),
        "child_map": draw_child_map(jax.random.fold_in(keys[3], 71), 0),
    }


def row_slot(front_blocks):
    return front_blocks % NRW * RBD + front_blocks // NRW

def reference(front, children, child_map):
    col_ids = jnp.arange(NF, dtype=jnp.int32)
    owner_ids = col_ids // WCOL
    source_cols = owner_ids % NCL * (NSB * WCOL) + owner_ids // NCL * WCOL + col_ids % WCOL
    blocks = front.reshape(NB, BLK, NF)
    for child_id in range(KIDS):
        update = jnp.take(children[child_id], source_cols, axis=1).reshape(MB, BLK, NF)
        blocks = blocks.at[row_slot(child_map[child_id])].add(update)
    assembled = blocks.reshape(NF, NF)
    within = jnp.arange(BLK, dtype=jnp.int32)
    panel_ids = jnp.arange(PB, dtype=jnp.int32)
    panel_cols = (panel_ids[:, None] * WCOL + within[None, :]).reshape(PW)
    panel_rows = (row_slot(panel_ids)[:, None] * BLK + within[None, :]).reshape(PW)
    tall_panel = jnp.take(assembled, panel_cols, axis=1)
    corner = jnp.take(tall_panel, panel_rows, axis=0)
    factor = jnp.linalg.cholesky(0.5 * (corner + corner.T))
    lower = jax.scipy.linalg.solve_triangular(factor, tall_panel.T, lower=True).T
    lower = lower.at[panel_rows].set(factor)
    col_blocks = jnp.arange(NB, dtype=jnp.int32)
    front_cols = col_blocks % CBD * NCG + col_blocks // CBD
    col_rows = (row_slot(front_cols)[:, None] * BLK + within[None, :]).reshape(NF)
    across = jnp.take(lower, col_rows, axis=0)
    product = lax.dot_general(lower.astype(jnp.float32), across.astype(jnp.float32), (((1,), (1,)), ((), ())), precision=lax.Precision.HIGHEST, preferred_element_type=jnp.float32)
    keep_rows = jnp.ones((NF,), jnp.float32).at[panel_rows].set(0.0)
    result = (assembled - product) * keep_rows[:, None]
    return result.at[:, panel_cols].set(lower)
```

```python
import functools

import jax
import jax.numpy as jnp
from jax import lax
from jax.experimental import pallas as pl
from jax.experimental.pallas import tpu as pltpu
from jax.sharding import Mesh, PartitionSpec as P

BLK = 128
PB = 8
PW = PB * BLK
KIDS = 8
MBR = 2
NSB = 4
QR = BLK // NSB
f32 = jnp.float32
bf16 = jnp.bfloat16
NT = (((1,), (1,)), ((), ()))
NN = (((1,), (0,)), ((), ()))
SUB = ("yh", "core")
COL = ("yl", "x")
PLANE = SUB + COL
CHIPS = ("yh", "yl", "x")


def split(x):
    hi = x.astype(bf16)
    return hi, (x - hi.astype(f32)).astype(bf16)


def dot3(a, b, dims):
    (ah, al), (bh, bl) = a, b

    def dot(p, q):
        return lax.dot_general(p, q, dims, preferred_element_type=f32)

    return dot(ah, bh) + (dot(ah, bl) + dot(al, bh))


def row_of(x, j):
    return jnp.broadcast_to(x[j : j + 1, :], x.shape)


def col_of(x, j):
    return jnp.broadcast_to(x[:, j : j + 1], x.shape)


def factor_block(d):
    groups = BLK // 8
    rows = lax.broadcasted_iota(jnp.int32, (8, BLK), 0)
    lanes = lax.broadcasted_iota(jnp.int32, (8, BLK), 1)
    a = [d[8 * v : 8 * v + 8, :] for v in range(groups)]
    e = [(lanes == rows + 8 * v).astype(f32) for v in range(groups)]
    upper, inverse = [], []
    for p in range(groups):
        ap, ep = a[p], e[p]
        b = [col_of(ap, 8 * p + j) for j in range(8)]
        near = p + 1 < groups
        bn = [col_of(a[p + 1], 8 * p + j) for j in range(8)] if near else None
        us, es = [], []
        up = jnp.zeros((8, BLK), f32)
        ip = jnp.zeros((8, BLK), f32)
        for j in range(8):
            inv = lax.rsqrt(row_of(b[j], j))
            m = b[j] * inv
            u = row_of(ap, j) * inv
            w = row_of(ep, j) * inv
            us.append(u)
            es.append(w)
            up = jnp.where(rows == j, u, up)
            ip = jnp.where(rows == j, w, ip)
            if j < 7:
                ap = ap - m * u
                ep = ep - m * w
            if near:
                mn = bn[j] * inv
                a[p + 1] = a[p + 1] - mn * u
                e[p + 1] = e[p + 1] - mn * w
            for k in range(j + 1, 8):
                mk = row_of(m, k)
                b[k] = b[k] - m * mk
                if near:
                    bn[k] = bn[k] - mn * mk
        upper.append(up)
        inverse.append(ip)
        if p + 2 < groups:
            lt = up.T
            for v in range(p + 2, groups):
                lv = lt[8 * v : 8 * v + 8, :]
                av, ev = a[v], e[v]
                for j in range(8):
                    m = jnp.broadcast_to(lv[:, j : j + 1], (8, BLK))
                    av = av - m * us[j]
                    ev = ev - m * es[j]
                a[v], e[v] = av, ev
    return jnp.concatenate(upper, 0), jnp.concatenate(inverse, 0)


def corner_kernel(ids, own_ref, other_ref, piece_ref, xh_ref, xl_ref, c_ref, l_ref, lh_ref, ll_ref):
    nb = PB
    core, row, owner = ids[0], ids[1], ids[2]

    def at(i, n=1):
        return slice(i * BLK, (i + n) * BLK)

    for yh in range(2):
        for c in range(PB):
            for i in range(PB):
                base = i * BLK + yh * 2 * QR
                rows = slice(i * QR, (i + 1) * QR)
                c_ref[pl.ds(pl.multiple_of(base + core * QR, QR), QR), at(c)] = own_ref[yh * PB + c, rows, :]
                c_ref[pl.ds(pl.multiple_of(base + (1 - core) * QR, QR), QR), at(c)] = other_ref[yh * PB + c, rows, :]

    def sym(i, j):
        return 0.5 * (c_ref[at(i), at(j)] + c_ref[at(j), at(i)].T)

    def get(rows, cols):
        return lh_ref[rows, cols], ll_ref[rows, cols]

    def put(rows, cols, x):
        h, l = split(x)
        l_ref[rows, cols] = x
        lh_ref[rows, cols] = h
        ll_ref[rows, cols] = l
        return h, l

    def putx(rows, cols, x):
        h, l = split(x)
        xh_ref[rows, cols] = h
        xl_ref[rows, cols] = l

    r = lax.broadcasted_iota(jnp.int32, (BLK, BLK), 0)
    c = lax.broadcasted_iota(jnp.int32, (BLK, BLK), 1)
    d = sym(0, 0)
    zero = jnp.zeros((BLK, BLK), f32)
    zb = zero.astype(bf16)
    wp = panel = m = None
    for k in range(nb):
        below = nb - 1 - k
        cols = slice(0, k * BLK)
        if k >= 1:
            if below > 0:
                put(at(k + 1, below), at(k - 1), dot3(split(panel[BLK:]), wp, NT))
            if k >= 2:
                putx(at(k - 1), slice(0, (k - 1) * BLK), -dot3(wp, split(m), NN))
            m = dot3(get(at(k), cols), (xh_ref[cols, cols], xl_ref[cols, cols]), NN)
        if below > 0:
            panel = jnp.concatenate([sym(i, k) for i in range(k + 1, nb)], 0)
            dn = sym(k + 1, k + 1)
            if k >= 1:
                panel = panel - dot3(get(at(k + 1, below), cols), get(at(k), cols), NT)
                nx = get(at(k + 1), cols)
                dn = dn - dot3(nx, nx, NT)
        u, w = factor_block(d)
        l_ref[at(k), at(k)] = jnp.where(r >= c, u.T, zero)
        wp = split(w)
        xh_ref[at(k), at(k)], xl_ref[at(k), at(k)] = wp
        for j in range(k + 1, nb):
            l_ref[at(k), at(j)] = zero
            xh_ref[at(k), at(j)] = zb
            xl_ref[at(k), at(j)] = zb
        if below > 0:
            nxt = put(at(k + 1), at(k), dot3(split(panel[:BLK]), wp, NT))
            d = dn - dot3(nxt, nxt, NT)
    putx(at(nb - 1), slice(0, (nb - 1) * BLK), -dot3(wp, split(m), NN))
    place = pl.multiple_of(jnp.minimum(owner, PB - 1) * BLK, BLK)
    piece_ref[...] = l_ref[pl.ds(pl.multiple_of(row * BLK, BLK), BLK), pl.ds(place, BLK)]


def corner_step(ids, own, other):
    vm = pl.BlockSpec(memory_space=pltpu.VMEM)
    return pl.pallas_call(
        corner_kernel,
        out_shape=(
            jax.ShapeDtypeStruct((BLK, BLK), f32),
            jax.ShapeDtypeStruct((PW, PW), bf16),
            jax.ShapeDtypeStruct((PW, PW), bf16),
        ),
        in_specs=[pl.BlockSpec(memory_space=pltpu.SMEM), vm, vm],
        out_specs=[vm] * 3,
        scratch_shapes=[pltpu.VMEM((PW, PW), f32)] * 2 + [pltpu.VMEM((PW, PW), bf16)] * 2,
        compiler_params=pltpu.CompilerParams(vmem_limit_bytes=40 * 1024 * 1024),
        cost_estimate=pl.CostEstimate(flops=60_000_000_000, bytes_accessed=8 * PW * PW, transcendentals=PW),
        name="corner",
    )(ids, own, other)


def tail_kernel(ids, slots, front_ref, kids_ref, own_ref, other_ref, tc_ref, piece_ref, xh_ref, xl_ref, out_ref, th_ref, tl_ref, ch_ref, cl_ref):
    core, row, owner = ids[0], ids[1], ids[2]
    width = 2 * BLK

    def at(i, n=1):
        return slice(i * BLK, (i + n) * BLK)

    for yh in range(2):
        for c in range(PB):
            for which, ref in ((core, own_ref), (1 - core, other_ref)):
                for i in range(1, PB):
                    h, l = split(ref[yh * PB + c, (i - 1) * QR : i * QR, :])
                    rows = pl.ds(pl.multiple_of(i * BLK + yh * 2 * QR + which * QR, QR), QR)
                    th_ref[rows, at(c)] = h
                    tl_ref[rows, at(c)] = l
    for q in range(NSB):
        for c in range(PB):
            for g in range(2):
                h, l = split(tc_ref[q * PB + c, g * QR : (g + 1) * QR, :])
                rows = slice(g * BLK + q * QR, g * BLK + (q + 1) * QR)
                ch_ref[rows, at(c)] = h
                cl_ref[rows, at(c)] = l
    out_ref[...] = front_ref[...]
    for b in range(KIDS * MBR):
        rows = pl.ds(pl.multiple_of(slots[b] * BLK, BLK), BLK)
        out_ref[rows, :] += kids_ref[b]
    x = (xh_ref[...], xl_ref[...])
    y = dot3((ch_ref[...], cl_ref[...]), x, NT)
    z = split(dot3(split(y), x, NN))
    for i in range(1, PB):
        t = (th_ref[at(i), :], tl_ref[at(i), :])
        out_ref[at(i), :] -= dot3(t, z, NT)
    out_ref[at(0), :] = jnp.zeros((BLK, width), f32)

    @pl.when(owner < PB)
    def _():
        block = pl.ds(pl.multiple_of(jnp.minimum(owner, PB - 1) * BLK, BLK), BLK)
        xb = (xh_ref[block, :], xl_ref[block, :])
        out_ref[at(0), at(0)] = piece_ref[...]
        for i in range(1, PB):
            out_ref[at(i), at(0)] = dot3((th_ref[at(i), :], tl_ref[at(i), :]), xb, NT)


def tail_step(ids, slots, front, kids, own, other, tall_cols, piece, xh, xl):
    vm = pl.BlockSpec(memory_space=pltpu.VMEM)
    sm = pl.BlockSpec(memory_space=pltpu.SMEM)
    return pl.pallas_call(
        tail_kernel,
        out_shape=jax.ShapeDtypeStruct(front.shape, f32),
        in_specs=[sm, sm] + [vm] * 8,
        out_specs=vm,
        scratch_shapes=[pltpu.VMEM((PW, PW), bf16)] * 2 + [pltpu.VMEM((2 * BLK, PW), bf16)] * 2,
        compiler_params=pltpu.CompilerParams(vmem_limit_bytes=40 * 1024 * 1024),
        cost_estimate=pl.CostEstimate(flops=6_000_000_000, bytes_accessed=20 * PW * PW, transcendentals=0),
        name="tail",
    )(ids, slots, front, kids, own, other, tall_cols, piece, xh, xl)


def to_all(x, axes, count):
    return lax.all_to_all(jnp.broadcast_to(x[None], (count,) + x.shape), axes, 0, 0, tiled=True)


def other_core(x):
    return lax.ppermute(x, "core", [(0, 1), (1, 0)])


def local(front, children, child_map):
    row = lax.axis_index("row")
    sub = lax.axis_index(SUB)
    col = lax.axis_index(COL)
    owner = sub * PB + col
    ids = jnp.stack([lax.axis_index("core"), row, owner]).astype(jnp.int32)
    width = front.shape[1]
    mine = lax.dynamic_slice_in_dim(child_map, row * MBR, MBR, 1) // PB
    slots = mine.reshape(KIDS * MBR)
    here = lax.dynamic_slice_in_dim(mine, sub * 2, 2, 0).reshape(4)

    lead = children[:, :, :BLK].reshape(4, BLK, BLK)
    part = jnp.where(sub == 0, front[:BLK, :BLK], 0.0)
    for b in range(4):
        part = part + jnp.where(here[b] == 0, lead[b], 0.0)
    quarter = lax.all_to_all(part.reshape(NSB, QR, BLK), SUB, 0, 0, tiled=True).sum(0)
    column = to_all(quarter, "row", 8)
    c_own = to_all(column.reshape(8 * QR, BLK), CHIPS, 16)
    c_other = other_core(c_own)
    piece, xh, xl = corner_step(ids, c_own, c_other)

    kid_part = lead.reshape(4, NSB, QR, BLK).transpose(1, 0, 2, 3)
    front_part = front[:, :BLK].reshape(PB, NSB, QR, BLK).transpose(1, 0, 2, 3)
    came = lax.all_to_all(jnp.concatenate([kid_part, front_part], 1), SUB, 0, 0, tiled=True)
    onehot = (jnp.arange(PB, dtype=jnp.int32)[:, None] == slots[None, :]).astype(f32)
    summed = jnp.dot(
        onehot,
        came[:, :4].reshape(KIDS * MBR, QR * BLK),
        precision=lax.Precision.HIGHEST,
        preferred_element_type=f32,
    )
    tall = came[0, 4:] + summed.reshape(PB, QR, BLK)
    t_own = to_all(tall[1:].reshape(7 * QR, BLK), CHIPS, 16)
    t_other = other_core(t_own)
    along = to_all(tall, "row", 8).reshape(8, 2, NSB, QR, BLK)
    pieces = along.transpose(2, 0, 1, 3, 4).reshape(NSB * 8, 2 * QR, BLK)
    tall_cols = lax.all_to_all(pieces, PLANE, 0, 0, tiled=True)

    parts = children.reshape(2, MBR * BLK, NSB, width)
    kids = lax.all_to_all(parts, SUB, split_axis=2, concat_axis=0, tiled=True)
    kids = kids.reshape(KIDS * MBR, BLK, width)
    return tail_step(ids, slots, front, kids, t_own, t_other, tall_cols, piece, xh, xl)


def solution(mesh):
    fine = Mesh(mesh.devices.reshape(2, 2, 8, 2, 4), ("yh", "core", "row", "yl", "x"))
    placed = (P("row", PLANE), P(SUB, "row", COL), P())
    return jax.shard_map(
        local, mesh=fine, in_specs=placed, out_specs=P("row", PLANE), check_vma=False
    )
```

```python
import functools

import jax
import jax.numpy as jnp
from jax import lax
from jax.experimental import pallas as pl
from jax.experimental.pallas import tpu as pltpu
from jax.sharding import Mesh, PartitionSpec as P

BLK = 128
PB = 8
PW = PB * BLK
KIDS = 8
MBR = 2
NSB = 4
QR = BLK // NSB
f32 = jnp.float32
bf16 = jnp.bfloat16
NT = (((1,), (1,)), ((), ()))
NN = (((1,), (0,)), ((), ()))
SUB = ("yh", "core")
COL = ("yl", "x")
PLANE = SUB + COL
CHIPS = ("yh", "yl", "x")


def split(x):
    hi = x.astype(bf16)
    return hi, (x - hi.astype(f32)).astype(bf16)


def dot3(a, b, dims):
    (ah, al), (bh, bl) = a, b

    def dot(p, q):
        return lax.dot_general(p, q, dims, preferred_element_type=f32)

    return dot(ah, bh) + (dot(ah, bl) + dot(al, bh))


def row_of(x, j):
    return jnp.broadcast_to(x[j : j + 1, :], x.shape)


def col_of(x, j):
    return jnp.broadcast_to(x[:, j : j + 1], x.shape)


def thirds(x):
    h = x.astype(bf16).astype(f32)
    r = x - h
    m = r.astype(bf16).astype(f32)
    return h, m, r - m


def factor_block(d):
    groups, wide, near = BLK // 8, 2, 2
    rows = lax.broadcasted_iota(jnp.int32, (8, BLK), 0)
    lanes = lax.broadcasted_iota(jnp.int32, (8, BLK), 1)
    a = [d[8 * v : 8 * v + 8, :] for v in range(groups)]
    e = [(lanes == rows + 8 * v).astype(f32) for v in range(groups)]
    upper, inverse = [], []
    for p in range(0, groups, wide):
        last = min(p + wide + near, groups)
        b = {v: [col_of(a[v], 8 * p + j) for j in range(8 * wide)] for v in range(p, last)}
        up = [jnp.zeros((8, BLK), f32)] * wide
        ip = [jnp.zeros((8, BLK), f32)] * wide
        for j in range(0, 8 * wide, 2):
            i, s0 = j // 8, j % 8
            x, y = b[p + i][j], b[p + i][j + 1]
            pp, q, s = row_of(x, s0), row_of(x, s0 + 1), row_of(y, s0 + 1)
            det = pp * s - q * q
            rd = pltpu.reciprocal(det, approx=True)

            def solved(first, second):
                return s * first - q * second, pp * second - q * first

            a0, a1 = row_of(a[p + i], s0), row_of(a[p + i], s0 + 1)
            e0, e1 = row_of(e[p + i], s0), row_of(e[p + i], s0 + 1)
            r1 = lax.rsqrt(pp)
            r2 = r1 * lax.rsqrt(det)
            up[i] = jnp.where(rows == s0, a0 * r1, jnp.where(rows == s0 + 1, (pp * a1 - q * a0) * r2, up[i]))
            ip[i] = jnp.where(rows == s0, e0 * r1, jnp.where(rows == s0 + 1, (pp * e1 - q * e0) * r2, ip[i]))
            ca, ce = solved(a0, a1), solved(e0, e1)
            ca, ce = (ca[0] * rd, ca[1] * rd), (ce[0] * rd, ce[1] * rd)
            ck = {
                k: solved(row_of(b[p + k // 8][j], k % 8), row_of(b[p + k // 8][j + 1], k % 8))
                for k in range(j + 2, 8 * wide)
            }
            for v in range(p + (j + 2) // 8, last):
                xv, yv = b[v][j], b[v][j + 1]
                for k in range(j + 2, 8 * wide):
                    b[v][k] = b[v][k] - (xv * ck[k][0] + yv * ck[k][1]) * rd
                a[v] = a[v] - (xv * ca[0] + yv * ca[1])
                e[v] = e[v] - (xv * ce[0] + yv * ce[1])
        upper += up
        inverse += ip
        if last < groups:
            h, m, l = thirds(jnp.concatenate(up, 0))
            hi, mi, li = thirds(jnp.concatenate(ip, 0))
            lhs = jnp.concatenate([h, h, m, h, l, m], 0).T[8 * last :, :].astype(bf16)
            left, right = jnp.concatenate([h, m, h, l, h, m], 0), jnp.concatenate([hi, mi, hi, li, hi, mi], 0)
            rhs = jnp.concatenate([left, right], 1).astype(bf16)
            r = lax.dot_general(lhs, rhs, NN, preferred_element_type=f32)
            for v in range(last, groups):
                part = slice(8 * (v - last), 8 * (v - last) + 8)
                a[v] = a[v] - r[part, :BLK]
                e[v] = e[v] - r[part, BLK:]
    return jnp.concatenate(upper, 0), jnp.concatenate(inverse, 0)


def at(i, n=1):
    return slice(i * BLK, (i + n) * BLK)


def block_ds(i):
    return pl.ds(pl.multiple_of(i * BLK, BLK), BLK)


def vmem(count):
    return [pl.BlockSpec(memory_space=pltpu.VMEM)] * count


def hbm(count):
    return [pl.BlockSpec(memory_space=pltpu.HBM)] * count


def smem(count):
    return [pl.BlockSpec(memory_space=pltpu.SMEM)] * count


def steps(first, nb, d, sym, lh_ref, ll_ref, xh_ref, xl_ref, final=lambda k: None):
    r = lax.broadcasted_iota(jnp.int32, (BLK, BLK), 0)
    c = lax.broadcasted_iota(jnp.int32, (BLK, BLK), 1)
    zb = jnp.zeros((BLK, BLK), bf16)

    def get(rows, cols):
        return lh_ref[rows, cols], ll_ref[rows, cols]

    def getx(rows, cols):
        return xh_ref[rows, cols], xl_ref[rows, cols]

    def put(rows, cols, x):
        h, l = split(x)
        lh_ref[rows, cols] = h
        ll_ref[rows, cols] = l
        return h, l

    def putx(rows, cols, x):
        h, l = split(x)
        xh_ref[rows, cols] = h
        xl_ref[rows, cols] = l

    wp = panel = m = None

    def finish(k):
        if k + 2 < nb:
            put(at(k + 2, nb - 2 - k), at(k), dot3(split(panel[BLK:]), wp, NT))
        if k >= 1:
            putx(at(k), slice(0, k * BLK), -dot3(wp, split(m), NN))
        final(k)

    for k in range(first, nb):
        below = nb - 1 - k
        cols = slice(0, k * BLK)
        if k > first:
            finish(k - 1)
        if k >= 1:
            m = dot3(get(at(k), cols), getx(cols, cols), NN)
        if below > 0:
            panel = jnp.concatenate([sym(i, k) for i in range(k + 1, nb)], 0)
            dn = sym(k + 1, k + 1)
            if k >= 1:
                panel = panel - dot3(get(at(k + 1, below), cols), get(at(k), cols), NT)
                nx = get(at(k + 1), cols)
                dn = dn - dot3(nx, nx, NT)
        u, w = factor_block(d)
        put(at(k), at(k), jnp.where(r >= c, u.T, 0.0))
        wp = split(w)
        xh_ref[at(k), at(k)], xl_ref[at(k), at(k)] = wp
        for j in range(k + 1, nb):
            lh_ref[at(k), at(j)] = zb
            ll_ref[at(k), at(j)] = zb
            xh_ref[at(k), at(j)] = zb
            xl_ref[at(k), at(j)] = zb
        if below > 0:
            nxt = put(at(k + 1), at(k), dot3(split(panel[:BLK]), wp, NT))
            d = dn - dot3(nxt, nxt, NT)
    finish(nb - 1)


def assemble(core, own_ref, other_ref, c_ref):
    for yh in range(2):
        for c in range(PB):
            for i in range(PB):
                base = i * BLK + yh * 2 * QR
                rows = slice(i * QR, (i + 1) * QR)
                c_ref[pl.ds(pl.multiple_of(base + core * QR, QR), QR), at(c)] = own_ref[yh * PB + c, rows, :]
                c_ref[pl.ds(pl.multiple_of(base + (1 - core) * QR, QR), QR), at(c)] = other_ref[yh * PB + c, rows, :]


def symmetric(c_ref):
    def sym(i, j):
        return 0.5 * (c_ref[at(i), at(j)] + c_ref[at(j), at(i)].T)

    return sym


def corner_kernel(
    ids, own, other, piece_ref, xh_out, xl_out,
    own_ref, other_ref, lh_ref, ll_ref, xh_ref, xl_ref, c_ref, in_sems, out_sems,
):
    row, owner = ids[1], ids[2]
    copies = [pltpu.make_async_copy(own, own_ref, in_sems.at[0]), pltpu.make_async_copy(other, other_ref, in_sems.at[1])]
    for copy in copies:
        copy.start()
    for copy in copies:
        copy.wait()
    assemble(ids[0], own_ref, other_ref, c_ref)
    sym = symmetric(c_ref)
    sent = []

    def send(k):
        for src, dst in ((xh_ref, xh_out), (xl_ref, xl_out)):
            copy = pltpu.make_async_copy(src.at[at(k), :], dst.at[at(k), :], out_sems.at[len(sent)])
            copy.start()
            sent.append(copy)

    steps(0, PB, sym(0, 0), sym, lh_ref, ll_ref, xh_ref, xl_ref, send)
    rows, cols = block_ds(row), block_ds(jnp.minimum(owner, PB - 1))
    piece_ref[...] = lh_ref[rows, cols].astype(f32) + ll_ref[rows, cols].astype(f32)
    for copy in sent:
        copy.wait()


HALF = jax.ShapeDtypeStruct((PW, PW), bf16)
BLOCK = jax.ShapeDtypeStruct((BLK, BLK), f32)
PARAMS = pltpu.CompilerParams(vmem_limit_bytes=60 * 1024 * 1024)


def corner_step(ids, own, other):
    return pl.pallas_call(
        corner_kernel,
        out_shape=(BLOCK, HALF, HALF),
        in_specs=smem(1) + hbm(2),
        out_specs=vmem(1) + hbm(2),
        scratch_shapes=[pltpu.VMEM(own.shape, f32)] * 2
        + [pltpu.VMEM((PW, PW), bf16)] * 4
        + [pltpu.VMEM((PW, PW), f32), pltpu.SemaphoreType.DMA((2,)), pltpu.SemaphoreType.DMA((2 * PB,))],
        compiler_params=PARAMS,
        cost_estimate=pl.CostEstimate(flops=35_000_000_000, bytes_accessed=8 * PW * PW, transcendentals=PW),
        name="corner",
    )(ids, own, other)


def right_kernel(ids, tc_ref, xh, xl, zh_ref, zl_ref, xh_ref, xl_ref, ch_ref, cl_ref, sems):
    copies = [pltpu.make_async_copy(xh, xh_ref, sems.at[0]), pltpu.make_async_copy(xl, xl_ref, sems.at[1])]
    for copy in copies:
        copy.start()
    for q in range(NSB):
        for c in range(PB):
            for g in range(2):
                h, l = split(tc_ref[q * PB + c, g * QR : (g + 1) * QR, :])
                rows = slice(g * BLK + q * QR, g * BLK + (q + 1) * QR)
                ch_ref[rows, at(c)] = h
                cl_ref[rows, at(c)] = l
    for copy in copies:
        copy.wait()
    ys = []
    for i in range(4):
        rows, cols = at(2 * i, 2), slice(0, (2 * i + 2) * BLK)
        ys.append(dot3((ch_ref[:, cols], cl_ref[:, cols]), (xh_ref[rows, cols], xl_ref[rows, cols]), NT))
    yh, yl = split(jnp.concatenate(ys, 1))
    for i in range(4):
        rows, cols = slice(2 * i * BLK, PW), at(2 * i, 2)
        h, l = split(dot3((yh[:, rows], yl[:, rows]), (xh_ref[rows, cols], xl_ref[rows, cols]), NN))
        zh_ref[:, cols] = h
        zl_ref[:, cols] = l


def right_step(ids, tall_cols, xh, xl):
    return pl.pallas_call(
        right_kernel,
        out_shape=(jax.ShapeDtypeStruct((2 * BLK, PW), bf16),) * 2,
        in_specs=smem(1) + vmem(1) + hbm(2),
        out_specs=vmem(2),
        scratch_shapes=[pltpu.VMEM((PW, PW), bf16)] * 2
        + [pltpu.VMEM((2 * BLK, PW), bf16)] * 2
        + [pltpu.SemaphoreType.DMA((2,))],
        compiler_params=PARAMS,
        cost_estimate=pl.CostEstimate(flops=4_000_000_000, bytes_accessed=8 * PW * PW, transcendentals=0),
        name="right",
    )(ids, tall_cols, xh, xl)


def tail_kernel(
    ids, child_map, front, k0, k1, k2, k3, own, other, piece_ref, zh_ref, zl_ref, xh, xl, out_ref,
    k0_ref, k1_ref, k2_ref, k3_ref, own_ref, other_ref, xh_ref, xl_ref, th_ref, tl_ref, sems,
):
    core, row, owner, sub = ids[0], ids[1], ids[2], ids[3]
    block = block_ds(jnp.minimum(owner, PB - 1))
    pairs = [(own, own_ref), (other, other_ref), (front, out_ref)]
    pairs += [(k0, k0_ref), (k1, k1_ref), (k2, k2_ref), (k3, k3_ref)]
    pairs += [(xh.at[block, :], xh_ref), (xl.at[block, :], xl_ref)]
    copies = [pltpu.make_async_copy(src, dst, sems.at[i]) for i, (src, dst) in enumerate(pairs)]
    for copy in copies:
        copy.start()
    for n, (which, ref) in enumerate(((core, own_ref), (1 - core, other_ref))):
        copies[n].wait()
        for yh in range(2):
            for c in range(PB):
                for i in range(1, PB):
                    h, l = split(ref[yh * PB + c, (i - 1) * QR : i * QR, :])
                    rows = pl.ds(pl.multiple_of(i * BLK + yh * 2 * QR + which * QR, QR), QR)
                    th_ref[rows, at(c)] = h
                    tl_ref[rows, at(c)] = l
    for copy in copies[2:]:
        copy.wait()
    for k, ref in enumerate((k0_ref, k1_ref, k2_ref, k3_ref)):
        for b in range(4):
            slot = child_map[(sub ^ k) * 2 + b // 2, row * MBR + b % 2] >> 3
            out_ref[block_ds(slot), :] += ref[at(b), :]
    rest = at(1, PB - 1)
    tall = (th_ref[rest, :], tl_ref[rest, :])
    out_ref[rest, :] -= dot3(tall, (zh_ref[...], zl_ref[...]), NT)
    out_ref[at(0), :] = jnp.zeros((BLK, 2 * BLK), f32)

    @pl.when(owner < PB)
    def _():
        out_ref[at(0), at(0)] = piece_ref[...]
        out_ref[rest, at(0)] = dot3((th_ref[rest, :], tl_ref[rest, :]), (xh_ref[...], xl_ref[...]), NT)


def tail_step(ids, child_map, front, kids, own, other, piece, right, xh, xl):
    landed = [*kids, own, other]
    return pl.pallas_call(
        tail_kernel,
        out_shape=jax.ShapeDtypeStruct(front.shape, f32),
        in_specs=smem(2) + hbm(7) + vmem(3) + hbm(2),
        out_specs=vmem(1)[0],
        scratch_shapes=[pltpu.VMEM(x.shape, x.dtype) for x in landed]
        + [pltpu.VMEM((BLK, PW), bf16)] * 2
        + [pltpu.VMEM((PW, PW), bf16)] * 2
        + [pltpu.SemaphoreType.DMA((9,))],
        compiler_params=PARAMS,
        cost_estimate=pl.CostEstimate(flops=4_000_000_000, bytes_accessed=20 * PW * PW, transcendentals=0),
        name="tail",
    )(ids, child_map, front, *kids, own, other, piece, *right, xh, xl)


ORDER = (0, 4, 2, 6, 1, 5, 3, 7)


def arrange_kernel(ids, mine_ref, came_ref, out_ref):
    row = ids[1]
    for i, k in enumerate(ORDER):
        ref = (mine_ref, came_ref)[i // 4]
        for s in range(NSB):
            for g in range(2):
                out_ref[pl.ds(s * PB + (row ^ k), 1), g * QR : (g + 1) * QR, :] = ref[i % 4, g * NSB + s][None]


def arrange(ids, mine, came):
    return pl.pallas_call(
        arrange_kernel,
        out_shape=jax.ShapeDtypeStruct((NSB * PB, 2 * QR, BLK), f32),
        in_specs=smem(1) + vmem(2),
        out_specs=vmem(1)[0],
        compiler_params=PARAMS,
        cost_estimate=pl.CostEstimate(flops=0, bytes_accessed=2 * PW * PW, transcendentals=0),
        name="arrange",
    )(ids, mine, came)


def prep_kernel(ids, front, children, p0, p1, p2, p3, lead_ref, front_ref, sems):
    sub = ids[3]
    copies = [
        pltpu.make_async_copy(children.at[:, :, at(0)], lead_ref, sems.at[0]),
        pltpu.make_async_copy(front.at[:, at(0)], front_ref, sems.at[1]),
    ]
    for copy in copies:
        copy.start()
    for copy in copies:
        copy.wait()
    for k, out_ref in enumerate((p0, p1, p2, p3)):
        quarter = (sub ^ k) * QR
        for b in range(4):
            out_ref[b] = lead_ref[b // 2, pl.ds(pl.multiple_of(b % 2 * BLK + quarter, QR), QR), :]
        for i in range(PB):
            out_ref[4 + i] = front_ref[pl.ds(pl.multiple_of(i * BLK + quarter, QR), QR), :]


def prepare(ids, front, children):
    return pl.pallas_call(
        prep_kernel,
        out_shape=(jax.ShapeDtypeStruct((4 + PB, QR, BLK), f32),) * 4,
        in_specs=smem(1) + hbm(2),
        out_specs=vmem(4),
        scratch_shapes=[
            pltpu.VMEM(children.shape[:2] + (BLK,), f32),
            pltpu.VMEM((front.shape[0], BLK), f32),
            pltpu.SemaphoreType.DMA((2,)),
        ],
        compiler_params=PARAMS,
        cost_estimate=pl.CostEstimate(flops=0, bytes_accessed=2 * PW * PW, transcendentals=0),
        name="prepare",
    )(ids, front, children)


def tall_kernel(ids, child_map, c0, c1, c2, c3, out_ref, rest_ref):
    row, sub = ids[1], ids[3]
    came = (c0, c1, c2, c3)
    total = c0[4:]
    for k in range(1, NSB):
        total = jnp.where(sub == k, came[k][4:], total)
    out_ref[...] = total
    for k in range(NSB):
        for b in range(4):
            slot = child_map[(sub ^ k) * 2 + b // 2, row * MBR + b % 2] >> 3
            out_ref[pl.ds(slot, 1)] += came[k][b][None]
    rest_ref[...] = out_ref[1:].reshape(rest_ref.shape)


def tall_quarter(ids, child_map, came):
    return pl.pallas_call(
        tall_kernel,
        out_shape=(jax.ShapeDtypeStruct((PB, QR, BLK), f32), jax.ShapeDtypeStruct(((PB - 1) * QR, BLK), f32)),
        in_specs=smem(2) + vmem(4),
        out_specs=vmem(2),
        compiler_params=PARAMS,
        cost_estimate=pl.CostEstimate(flops=0, bytes_accessed=PW * PW, transcendentals=0),
        name="tall",
    )(ids, child_map, *came)


def to_all(x, axes, count):
    return lax.all_to_all(jnp.broadcast_to(x[None], (count,) + x.shape), axes, 0, 0, tiled=True)


def flip(x, axes, count, k):
    return lax.ppermute(x, axes, [(i, i ^ k) for i in range(count)])


def local(front, children, child_map):
    row = lax.axis_index("row")
    sub = lax.axis_index(SUB)
    owner = sub * PB + lax.axis_index(COL)
    ids = jnp.stack([lax.axis_index("core"), row, owner, sub]).astype(jnp.int32)
    width = front.shape[1]

    pieces = prepare(ids, front, children)
    came = pieces[:1] + tuple(flip(pieces[k], SUB, NSB, k) for k in range(1, NSB))
    tall, tall_rest = tall_quarter(ids, child_map, came)

    column = to_all(tall[0], "row", 8)
    t_own = lax.all_gather(tall_rest, CHIPS, axis=0, tiled=False)
    along = jnp.stack([tall, flip(tall, "row", 8, 4)])
    column, along = lax.optimization_barrier((column, along))
    along = jnp.concatenate([along, flip(along, "row", 8, 2)])
    along_came = flip(along, "row", 8, 1)

    c_own = to_all(column.reshape(8 * QR, BLK), CHIPS, 16)
    c_own, along, along_came = lax.optimization_barrier((c_own, along, along_came))
    c_other = flip(c_own, "core", 2, 1)
    tall_cols = lax.all_to_all(arrange(ids, along, along_came), PLANE, 0, 0, tiled=True)

    kids = []
    for k in range(NSB):
        piece = lax.dynamic_slice_in_dim(children, (sub ^ k) * width, width, 2).reshape(4 * BLK, width)
        kids.append(flip(piece, SUB, NSB, k) if k else piece)
    piece, xh, xl = corner_step(ids, c_own, c_other)
    xh, xl, *kids = lax.optimization_barrier((xh, xl, *kids))
    right = right_step(ids, tall_cols, xh, xl)
    t_own, *right = lax.optimization_barrier((t_own, *right))
    t_other = flip(t_own, "core", 2, 1)
    return tail_step(ids, child_map, front, kids, t_own, t_other, piece, right, xh, xl)


def solution(mesh):
    fine = Mesh(mesh.devices.reshape(2, 2, 8, 2, 4), ("yh", "core", "row", "yl", "x"))
    placed = (P("row", PLANE), P(SUB, "row", COL), P())
    return jax.shard_map(
        local, mesh=fine, in_specs=placed, out_specs=P("row", PLANE), check_vma=False
    )
```

```python
import functools

import jax
import jax.numpy as jnp
from jax import lax
from jax.experimental import pallas as pl
from jax.experimental.pallas import tpu as pltpu
from jax.sharding import Mesh, PartitionSpec as P

BLK = 128
PB = 8
PW = PB * BLK
KIDS = 8
MBR = 2
NSB = 4
QR = BLK // NSB
f32 = jnp.float32
bf16 = jnp.bfloat16
NT = (((1,), (1,)), ((), ()))
NN = (((1,), (0,)), ((), ()))
SUB = ("yh", "core")
COL = ("yl", "x")
PLANE = SUB + COL
CHIPS = ("yh", "yl", "x")


def split(x):
    hi = x.astype(bf16)
    return hi, (x - hi.astype(f32)).astype(bf16)


def dot3(a, b, dims):
    (ah, al), (bh, bl) = a, b

    def dot(p, q):
        return lax.dot_general(p, q, dims, preferred_element_type=f32)

    return dot(ah, bh) + (dot(ah, bl) + dot(al, bh))


def row_of(x, j):
    return jnp.broadcast_to(x[j : j + 1, :], x.shape)


def col_of(x, j):
    return jnp.broadcast_to(x[:, j : j + 1], x.shape)


def thirds(x):
    h = x.astype(bf16).astype(f32)
    r = x - h
    m = r.astype(bf16).astype(f32)
    return h, m, r - m


def factor_block(d, work=()):
    work = list(work)
    groups, wide, near = BLK // 8, 2, 2
    rows = lax.broadcasted_iota(jnp.int32, (8, BLK), 0)
    lanes = lax.broadcasted_iota(jnp.int32, (8, BLK), 1)
    a = [d[8 * v : 8 * v + 8, :] for v in range(groups)]
    e = [(lanes == rows + 8 * v).astype(f32) for v in range(groups)]
    upper, inverse = [], []
    for p in range(0, groups, wide):
        last = min(p + wide + near, groups)
        b = {v: [col_of(a[v], 8 * p + j) for j in range(8 * wide)] for v in range(p, last)}
        up = [jnp.zeros((8, BLK), f32)] * wide
        ip = [jnp.zeros((8, BLK), f32)] * wide
        for j in range(0, 8 * wide, 2):
            i, s0 = j // 8, j % 8
            x, y = b[p + i][j], b[p + i][j + 1]
            pp, q, s = row_of(x, s0), row_of(x, s0 + 1), row_of(y, s0 + 1)
            det = pp * s - q * q
            rd = pltpu.reciprocal(det, approx=True)

            def solved(first, second):
                return s * first - q * second, pp * second - q * first

            a0, a1 = row_of(a[p + i], s0), row_of(a[p + i], s0 + 1)
            e0, e1 = row_of(e[p + i], s0), row_of(e[p + i], s0 + 1)
            r1 = lax.rsqrt(pp)
            r2 = r1 * lax.rsqrt(det)
            up[i] = jnp.where(rows == s0, a0 * r1, jnp.where(rows == s0 + 1, (pp * a1 - q * a0) * r2, up[i]))
            ip[i] = jnp.where(rows == s0, e0 * r1, jnp.where(rows == s0 + 1, (pp * e1 - q * e0) * r2, ip[i]))
            ca, ce = solved(a0, a1), solved(e0, e1)
            ca, ce = (ca[0] * rd, ca[1] * rd), (ce[0] * rd, ce[1] * rd)
            ck = {
                k: solved(row_of(b[p + k // 8][j], k % 8), row_of(b[p + k // 8][j + 1], k % 8))
                for k in range(j + 2, 8 * wide)
            }
            for v in range(p + (j + 2) // 8, last):
                xv, yv = b[v][j], b[v][j + 1]
                for k in range(j + 2, 8 * wide):
                    b[v][k] = b[v][k] - (xv * ck[k][0] + yv * ck[k][1]) * rd
                a[v] = a[v] - (xv * ca[0] + yv * ca[1])
                e[v] = e[v] - (xv * ce[0] + yv * ce[1])
        upper += up
        inverse += ip
        if work:
            work.pop(0)()
        if last < groups:
            h, m, l = thirds(jnp.concatenate(up, 0))
            hi, mi, li = thirds(jnp.concatenate(ip, 0))
            lhs = jnp.concatenate([h, h, m, h, l, m], 0).T[8 * last :, :].astype(bf16)
            left, right = jnp.concatenate([h, m, h, l, h, m], 0), jnp.concatenate([hi, mi, hi, li, hi, mi], 0)
            rhs = jnp.concatenate([left, right], 1).astype(bf16)
            r = lax.dot_general(lhs, rhs, NN, preferred_element_type=f32)
            for v in range(last, groups):
                part = slice(8 * (v - last), 8 * (v - last) + 8)
                a[v] = a[v] - r[part, :BLK]
                e[v] = e[v] - r[part, BLK:]
    for call in work:
        call()
    return jnp.concatenate(upper, 0), jnp.concatenate(inverse, 0)


def at(i, n=1):
    return slice(i * BLK, (i + n) * BLK)


def block_ds(i):
    return pl.ds(pl.multiple_of(i * BLK, BLK), BLK)


def vmem(count):
    return [pl.BlockSpec(memory_space=pltpu.VMEM)] * count


def hbm(count):
    return [pl.BlockSpec(memory_space=pltpu.HBM)] * count


def smem(count):
    return [pl.BlockSpec(memory_space=pltpu.SMEM)] * count


def steps(first, nb, d, sym, lh_ref, ll_ref, xh_ref, xl_ref, final=lambda k: None):
    r = lax.broadcasted_iota(jnp.int32, (BLK, BLK), 0)
    c = lax.broadcasted_iota(jnp.int32, (BLK, BLK), 1)
    zb = jnp.zeros((BLK, BLK), bf16)

    def get(rows, cols):
        return lh_ref[rows, cols], ll_ref[rows, cols]

    def getx(rows, cols):
        return xh_ref[rows, cols], xl_ref[rows, cols]

    def put(rows, cols, x):
        h, l = split(x)
        lh_ref[rows, cols] = h
        ll_ref[rows, cols] = l
        return h, l

    def putx(rows, cols, x):
        h, l = split(x)
        xh_ref[rows, cols] = h
        xl_ref[rows, cols] = l

    wp = None
    panel, m = {}, {}

    def finish_column(k):
        if k + 2 < nb:
            low = jnp.concatenate([panel[i] for i in range(k + 2, nb)], 0)
            put(at(k + 2, nb - 2 - k), at(k), dot3(split(low), wp, NT))

    def finish_row(k):
        if k >= 1:
            putx(at(k), slice(0, k * BLK), -dot3(wp, split(jnp.concatenate([m[j] for j in sorted(m)], 1)), NN))
        final(k)

    def next_rows(k, i, n):
        part = jnp.concatenate([sym(j, k) for j in range(i, i + n)], 0)
        if k >= 1:
            cols = slice(0, k * BLK)
            part = part - dot3(get(at(i, n), cols), get(at(k), cols), NT)
        for j in range(n):
            panel[i + j] = part[at(j)]

    def next_block(k):
        block = sym(k + 1, k + 1)
        if k >= 1:
            nx = get(at(k + 1), slice(0, k * BLK))
            block = block - dot3(nx, nx, NT)
        panel["diagonal"] = block

    def row_product(k, j, n):
        cols = slice(j * BLK, k * BLK)
        m[j] = dot3(get(at(k), cols), getx(cols, at(j, n)), NN)

    def restart(k):
        finish_row(k - 1)
        m.clear()

    for k in range(first, nb):
        work = []
        if k > first:
            work += [functools.partial(finish_column, k - 1), functools.partial(restart, k)]
        if k + 1 < nb:
            work.append(functools.partial(next_block, k))
        groups = [functools.partial(next_rows, k, i, min(3, nb - i)) for i in range(k + 1, nb, 3)]
        groups += [functools.partial(row_product, k, j, min(3, k - j)) for j in range(0, k, 3)]
        u, w = factor_block(d, work + groups)
        put(at(k), at(k), jnp.where(r >= c, u.T, 0.0))
        wp = split(w)
        xh_ref[at(k), at(k)], xl_ref[at(k), at(k)] = wp
        for j in range(k + 1, nb):
            lh_ref[at(k), at(j)] = zb
            ll_ref[at(k), at(j)] = zb
            xh_ref[at(k), at(j)] = zb
            xl_ref[at(k), at(j)] = zb
        if k + 1 < nb:
            nxt = put(at(k + 1), at(k), dot3(split(panel[k + 1]), wp, NT))
            d = panel["diagonal"] - dot3(nxt, nxt, NT)
    finish_row(nb - 1)


def assemble(core, own_ref, other_ref, c_ref):
    for yh in range(2):
        for c in range(PB):
            for i in range(PB):
                base = i * BLK + yh * 2 * QR
                rows = slice(i * QR, (i + 1) * QR)
                c_ref[pl.ds(pl.multiple_of(base + core * QR, QR), QR), at(c)] = own_ref[yh * PB + c, rows, :]
                c_ref[pl.ds(pl.multiple_of(base + (1 - core) * QR, QR), QR), at(c)] = other_ref[yh * PB + c, rows, :]


def symmetric(c_ref):
    def sym(i, j):
        return 0.5 * (c_ref[at(i), at(j)] + c_ref[at(j), at(i)].T)

    return sym


def corner_kernel(
    ids, own, other, piece_ref, xh_out, xl_out,
    own_ref, other_ref, lh_ref, ll_ref, xh_ref, xl_ref, c_ref, in_sems, out_sems,
):
    row, owner = ids[1], ids[2]
    copies = [pltpu.make_async_copy(own, own_ref, in_sems.at[0]), pltpu.make_async_copy(other, other_ref, in_sems.at[1])]
    for copy in copies:
        copy.start()
    for copy in copies:
        copy.wait()
    assemble(ids[0], own_ref, other_ref, c_ref)
    sym = symmetric(c_ref)
    sent = []

    def send(k):
        for src, dst in ((xh_ref, xh_out), (xl_ref, xl_out)):
            copy = pltpu.make_async_copy(src.at[at(k), :], dst.at[at(k), :], out_sems.at[len(sent)])
            copy.start()
            sent.append(copy)

    steps(0, PB, sym(0, 0), sym, lh_ref, ll_ref, xh_ref, xl_ref, send)
    rows, cols = block_ds(row), block_ds(jnp.minimum(owner, PB - 1))
    piece_ref[...] = lh_ref[rows, cols].astype(f32) + ll_ref[rows, cols].astype(f32)
    for copy in sent:
        copy.wait()


HALF = jax.ShapeDtypeStruct((PW, PW), bf16)
BLOCK = jax.ShapeDtypeStruct((BLK, BLK), f32)
PARAMS = pltpu.CompilerParams(vmem_limit_bytes=60 * 1024 * 1024)


def corner_step(ids, own, other):
    return pl.pallas_call(
        corner_kernel,
        out_shape=(BLOCK, HALF, HALF),
        in_specs=smem(1) + hbm(2),
        out_specs=vmem(1) + hbm(2),
        scratch_shapes=[pltpu.VMEM(own.shape, f32)] * 2
        + [pltpu.VMEM((PW, PW), bf16)] * 4
        + [pltpu.VMEM((PW, PW), f32), pltpu.SemaphoreType.DMA((2,)), pltpu.SemaphoreType.DMA((2 * PB,))],
        compiler_params=PARAMS,
        cost_estimate=pl.CostEstimate(flops=35_000_000_000, bytes_accessed=8 * PW * PW, transcendentals=PW),
        name="corner",
    )(ids, own, other)


def right_kernel(ids, tc_ref, xh, xl, zh_ref, zl_ref, xh_ref, xl_ref, ch_ref, cl_ref, sems):
    copies = [pltpu.make_async_copy(xh, xh_ref, sems.at[0]), pltpu.make_async_copy(xl, xl_ref, sems.at[1])]
    for copy in copies:
        copy.start()
    for q in range(NSB):
        for c in range(PB):
            for g in range(2):
                h, l = split(tc_ref[q * PB + c, g * QR : (g + 1) * QR, :])
                rows = slice(g * BLK + q * QR, g * BLK + (q + 1) * QR)
                ch_ref[rows, at(c)] = h
                cl_ref[rows, at(c)] = l
    for copy in copies:
        copy.wait()
    ys = []
    for i in range(4):
        rows, cols = at(2 * i, 2), slice(0, (2 * i + 2) * BLK)
        ys.append(dot3((ch_ref[:, cols], cl_ref[:, cols]), (xh_ref[rows, cols], xl_ref[rows, cols]), NT))
    yh, yl = split(jnp.concatenate(ys, 1))
    for i in range(4):
        rows, cols = slice(2 * i * BLK, PW), at(2 * i, 2)
        h, l = split(dot3((yh[:, rows], yl[:, rows]), (xh_ref[rows, cols], xl_ref[rows, cols]), NN))
        zh_ref[:, cols] = h
        zl_ref[:, cols] = l


def right_step(ids, tall_cols, xh, xl):
    return pl.pallas_call(
        right_kernel,
        out_shape=(jax.ShapeDtypeStruct((2 * BLK, PW), bf16),) * 2,
        in_specs=smem(1) + vmem(1) + hbm(2),
        out_specs=vmem(2),
        scratch_shapes=[pltpu.VMEM((PW, PW), bf16)] * 2
        + [pltpu.VMEM((2 * BLK, PW), bf16)] * 2
        + [pltpu.SemaphoreType.DMA((2,))],
        compiler_params=PARAMS,
        cost_estimate=pl.CostEstimate(flops=4_000_000_000, bytes_accessed=8 * PW * PW, transcendentals=0),
        name="right",
    )(ids, tall_cols, xh, xl)


def tail_kernel(
    ids, child_map, front, k0, k1, k2, k3, own0, own1, other0, other1, piece_ref, zh_ref, zl_ref, xh, xl, out_ref,
    k0_ref, k1_ref, k2_ref, k3_ref, own0_ref, own1_ref, other0_ref, other1_ref, xh_ref, xl_ref, th_ref, tl_ref, sems,
):
    row, owner, sub = ids[1], ids[2], ids[3]
    col = owner - sub * PB
    block = block_ds(jnp.minimum(owner, PB - 1))
    pairs = [(own0, own0_ref), (own1, own1_ref), (other0, other0_ref), (other1, other1_ref), (front, out_ref)]
    pairs += [(k0, k0_ref), (k1, k1_ref), (k2, k2_ref), (k3, k3_ref)]
    pairs += [(xh.at[block, :], xh_ref), (xl.at[block, :], xl_ref)]
    copies = [pltpu.make_async_copy(src, dst, sems.at[i]) for i, (src, dst) in enumerate(pairs)]
    for copy in copies:
        copy.start()
    for n, ref in enumerate((own0_ref, own1_ref, other0_ref, other1_ref)):
        copies[n].wait()
        which, dyl = n // 2, n % 2
        for dyh in range(2):
            quarter = (sub ^ (2 * dyh + which)) * QR
            for x in range(4):
                cols = block_ds(((col >> 2) ^ dyl) * 4 + x)
                for i in range(1, PB):
                    h, l = split(ref[dyh * 4 + x, (i - 1) * QR : i * QR, :])
                    rows = pl.ds(pl.multiple_of(i * BLK + quarter, QR), QR)
                    th_ref[rows, cols] = h
                    tl_ref[rows, cols] = l
    for copy in copies[4:]:
        copy.wait()
    for k, ref in enumerate((k0_ref, k1_ref, k2_ref, k3_ref)):
        for b in range(4):
            slot = child_map[(sub ^ k) * 2 + b // 2, row * MBR + b % 2] >> 3
            out_ref[block_ds(slot), :] += ref[at(b), :]
    rest = at(1, PB - 1)
    tall = (th_ref[rest, :], tl_ref[rest, :])
    out_ref[rest, :] -= dot3(tall, (zh_ref[...], zl_ref[...]), NT)
    out_ref[at(0), :] = jnp.zeros((BLK, 2 * BLK), f32)

    @pl.when(owner < PB)
    def _():
        out_ref[at(0), at(0)] = piece_ref[...]
        out_ref[rest, at(0)] = dot3((th_ref[rest, :], tl_ref[rest, :]), (xh_ref[...], xl_ref[...]), NT)


def tail_step(ids, child_map, front, kids, panel, piece, right, xh, xl):
    landed = [*kids, *panel]
    return pl.pallas_call(
        tail_kernel,
        out_shape=jax.ShapeDtypeStruct(front.shape, f32),
        in_specs=smem(2) + hbm(9) + vmem(3) + hbm(2),
        out_specs=vmem(1)[0],
        scratch_shapes=[pltpu.VMEM(x.shape, x.dtype) for x in landed]
        + [pltpu.VMEM((BLK, PW), bf16)] * 2
        + [pltpu.VMEM((PW, PW), bf16)] * 2
        + [pltpu.SemaphoreType.DMA((11,))],
        compiler_params=PARAMS,
        cost_estimate=pl.CostEstimate(flops=4_000_000_000, bytes_accessed=20 * PW * PW, transcendentals=0),
        name="tail",
    )(ids, child_map, front, *kids, *panel, piece, *right, xh, xl)


ORDER = (0, 4, 2, 6, 1, 5, 3, 7)


def arrange_kernel(ids, mine_ref, came_ref, out_ref):
    row = ids[1]
    for i, k in enumerate(ORDER):
        ref = (mine_ref, came_ref)[i // 4]
        for s in range(NSB):
            for g in range(2):
                out_ref[pl.ds(s * PB + (row ^ k), 1), g * QR : (g + 1) * QR, :] = ref[i % 4, g * NSB + s][None]


def arrange(ids, mine, came):
    return pl.pallas_call(
        arrange_kernel,
        out_shape=jax.ShapeDtypeStruct((NSB * PB, 2 * QR, BLK), f32),
        in_specs=smem(1) + vmem(2),
        out_specs=vmem(1)[0],
        compiler_params=PARAMS,
        cost_estimate=pl.CostEstimate(flops=0, bytes_accessed=2 * PW * PW, transcendentals=0),
        name="arrange",
    )(ids, mine, came)


def prep_kernel(ids, front, children, p0, p1, p2, p3, lead_ref, front_ref, sems):
    sub = ids[3]
    copies = [
        pltpu.make_async_copy(children.at[:, :, at(0)], lead_ref, sems.at[0]),
        pltpu.make_async_copy(front.at[:, at(0)], front_ref, sems.at[1]),
    ]
    for copy in copies:
        copy.start()
    for copy in copies:
        copy.wait()
    for k, out_ref in enumerate((p0, p1, p2, p3)):
        quarter = (sub ^ k) * QR
        for b in range(4):
            out_ref[b] = lead_ref[b // 2, pl.ds(pl.multiple_of(b % 2 * BLK + quarter, QR), QR), :]
        for i in range(PB):
            out_ref[4 + i] = front_ref[pl.ds(pl.multiple_of(i * BLK + quarter, QR), QR), :]


def prepare(ids, front, children):
    return pl.pallas_call(
        prep_kernel,
        out_shape=(jax.ShapeDtypeStruct((4 + PB, QR, BLK), f32),) * 4,
        in_specs=smem(1) + hbm(2),
        out_specs=vmem(4),
        scratch_shapes=[
            pltpu.VMEM(children.shape[:2] + (BLK,), f32),
            pltpu.VMEM((front.shape[0], BLK), f32),
            pltpu.SemaphoreType.DMA((2,)),
        ],
        compiler_params=PARAMS,
        cost_estimate=pl.CostEstimate(flops=0, bytes_accessed=2 * PW * PW, transcendentals=0),
        name="prepare",
    )(ids, front, children)


def tall_kernel(ids, child_map, c0, c1, c2, c3, out_ref, rest_ref):
    row, sub = ids[1], ids[3]
    came = (c0, c1, c2, c3)
    total = c0[4:]
    for k in range(1, NSB):
        total = jnp.where(sub == k, came[k][4:], total)
    out_ref[...] = total
    for k in range(NSB):
        for b in range(4):
            slot = child_map[(sub ^ k) * 2 + b // 2, row * MBR + b % 2] >> 3
            out_ref[pl.ds(slot, 1)] += came[k][b][None]
    rest_ref[...] = out_ref[1:].reshape(rest_ref.shape)


def tall_quarter(ids, child_map, came):
    return pl.pallas_call(
        tall_kernel,
        out_shape=(jax.ShapeDtypeStruct((PB, QR, BLK), f32), jax.ShapeDtypeStruct(((PB - 1) * QR, BLK), f32)),
        in_specs=smem(2) + vmem(4),
        out_specs=vmem(2),
        compiler_params=PARAMS,
        cost_estimate=pl.CostEstimate(flops=0, bytes_accessed=PW * PW, transcendentals=0),
        name="tall",
    )(ids, child_map, *came)


def to_all(x, axes, count):
    return lax.all_to_all(jnp.broadcast_to(x[None], (count,) + x.shape), axes, 0, 0, tiled=True)


def flip(x, axes, count, k):
    return lax.ppermute(x, axes, [(i, i ^ k) for i in range(count)])


def local(front, children, child_map):
    row = lax.axis_index("row")
    sub = lax.axis_index(SUB)
    owner = sub * PB + lax.axis_index(COL)
    ids = jnp.stack([lax.axis_index("core"), row, owner, sub]).astype(jnp.int32)
    width = front.shape[1]

    pieces = prepare(ids, front, children)
    came = pieces[:1] + tuple(flip(pieces[k], SUB, NSB, k) for k in range(1, NSB))
    tall, tall_rest = tall_quarter(ids, child_map, came)

    kids = []
    for k in range(NSB):
        piece = lax.dynamic_slice_in_dim(children, (sub ^ k) * width, width, 2).reshape(4 * BLK, width)
        kids.append(flip(piece, SUB, NSB, k) if k else piece)
    column = to_all(tall[0], "row", 8)
    t_own = lax.all_gather(tall_rest, "x", axis=0, tiled=False)
    along = jnp.stack([tall, flip(tall, "row", 8, 4)])
    column, along, t_own, *kids = lax.optimization_barrier((column, along, t_own, *kids))
    t_own = jnp.concatenate([t_own, flip(t_own, "yh", 2, 1)])
    along = jnp.concatenate([along, flip(along, "row", 8, 2)])
    along_came = flip(along, "row", 8, 1)

    c_own = to_all(column.reshape(8 * QR, BLK), CHIPS, 16)
    c_own, along, along_came, t_own = lax.optimization_barrier((c_own, along, along_came, t_own))
    t_came = flip(t_own, "yl", 2, 1)
    c_other = flip(c_own, "core", 2, 1)
    tall_cols = lax.all_to_all(arrange(ids, along, along_came), PLANE, 0, 0, tiled=True)

    piece, xh, xl = corner_step(ids, c_own, c_other)
    xh, xl, tall_cols = lax.optimization_barrier((xh, xl, tall_cols))
    right = right_step(ids, tall_cols, xh, xl)
    t_came, *right = lax.optimization_barrier((t_came, *right))
    panel = [t_own, t_came, flip(t_own, "core", 2, 1), flip(t_came, "core", 2, 1)]
    return tail_step(ids, child_map, front, kids, panel, piece, right, xh, xl)


def solution(mesh):
    fine = Mesh(mesh.devices.reshape(2, 2, 8, 2, 4), ("yh", "core", "row", "yl", "x"))
    placed = (P("row", PLANE), P(SUB, "row", COL), P())
    return jax.shard_map(
        local, mesh=fine, in_specs=placed, out_specs=P("row", PLANE), check_vma=False
    )
```
